32 devices in a mesh: table: 32 (over z, y, x, core), dp: 1.
Axes of the slice: x: 2, y: 2, z: 4, core: 2. Of those that a mesh axis runs over, the one named last changes fastest.
Arguments:
- table: bfloat16 [12288, 512], P('table'), may hold values from -6 to 6
- owner: int32 [32, 256, 1], P(('table', 'dp')), may hold values from 0 to 31; in each aligned block of 256 rows (0 to 255, 256 to 511, ..., all dimensions but the last counted through in order) at most 16 rows name the same one
- row_in_shard: int32 [32, 256], P(('table', 'dp')), may hold values from 0 to 383
- segment: int32 [32, 256], P(('table', 'dp')), may hold values from 0 to 3, never falling along the last dimension, each value on 1 to 128 neighbouring positions
- w_in: bfloat16 [512, 2048], replicated, may hold values from -0.25 to 0.25
- w_out: bfloat16 [512, 512], replicated, may hold values from -0.25 to 0.25
- cotangent: bfloat16 [32, 256, 512], P(('table', 'dp')), may hold values from -6 to 6
Outputs:
- layer_out: bfloat16 [32, 256, 512], P(('table', 'dp'))
- grad_table: float32 [12288, 512], P('table')
- grad_w_in: float32 [512, 2048], P(None, 'dp')
- grad_w_out: float32 [512, 512], P('dp')
The draws below stay inside these ranges and needn't reach their ends.
Inputs may be any that keep to these rules, and one draw needn't show every extreme that they name: `owner`: among one device's 256 positions no shard is named more than 16 times, a bound that some block reaches. `segment`: never falls along a buffer; each history has 1 to 128 positions and one has exactly 128.
All inputs are finite; a program needn't handle non-finite values.
Results may differ from the reference program's by a relative error of at most 0.019.
Values may be sent and summed in bfloat16 or wider, within the bound.
A program may use at most 64 MiB of HBM per device.

```python
import math
import jax
import jax.numpy as jnp
import numpy as np
from jax import lax

D = 512
HEADS = 8
ROWS = 256
NSEG = 4
VOCAB_DEV = 384
MOST = 128
CAP = 16
GROUPS = 32
VOCAB = 12288
N_TABLE = 32


def plant(values, own_key, low, high):
    extent = values.shape
    place = [jax.random.randint(jax.random.fold_in(own_key, axis), (), 0, extent[axis]) for axis in range(len(extent))]
    values = values.at[tuple(place)].set(low)
    longest = extent.index(max(extent))
    place[longest] = (place[longest] + 1) % extent[longest]
    return values.at[tuple(place)].set(high)


def block_levels(rng, dims, shards, low, largest):
    def one(dim, blocks):
        steps = jax.random.uniform(jax.random.fold_in(jax.random.fold_in(rng, 6), dim), (blocks,), jnp.float32, low / len(shards), largest / len(shards))
        return jnp.repeat(jnp.exp(steps), dims[dim] // blocks).reshape((-1,) + (1,) * (len(dims) - dim - 1))

    gain = one(*shards[0])
    for cut in shards[1:]:
        gain = gain * one(*cut)
    return gain


def length_profile(amount, total, limit, skew):
    portions = [(1 << 20) // math.isqrt(standing ** skew) + 1 for standing in range(2, amount + 1)]
    rest, given = total - limit - (amount - 1), [1] * (amount - 1)
    while rest > 0:
        free = [i for i in range(amount - 1) if given[i] < limit]
        mass, remaining = sum([portions[i] for i in free]), rest
        for i in free:
            addition = min(limit - given[i], max(1, remaining * portions[i] // mass), rest)
            given[i] = given[i] + addition
            rest = rest - addition
    return np.array([limit] + given)


def uneven(key, count, total, most, slope):
    if count == 2:
        one = jax.random.randint(key, (), max(1, total - most), min(most, total - 1) + 1)
        return jnp.stack([one, total - one])
    sizes = jnp.asarray(length_profile(count, total, most, slope), jnp.int32)
    twos = (count - 1) // 2
    source_of, receiver = sizes[1:1 + 2 * twos:2], sizes[2:2 + 2 * twos:2]
    room = jnp.minimum(source_of - 1, most - receiver)
    passed = jax.random.randint(jax.random.fold_in(key, 1), (twos,), 0, 1 << 20) % (room + 1)
    sizes = sizes.at[1:1 + 2 * twos:2].set(source_of - passed).at[2:2 + 2 * twos:2].set(receiver + passed)
    return sizes[jax.random.permutation(jax.random.fold_in(key, 2), count)]


def shared_out(key, own, number, rows, count, top, most, lean):
    order = jax.random.permutation(key, count)
    packed, common = portions_of(count, rows * top, most, lean, True), portions_of(count, rows * top, most, lean, False)
    places = jnp.arange(count)

    def named(tallies, rotation):
        used = int((tallies > 0).sum())
        fixed = max(1, used // 4)
        moved = fixed + (places - fixed + rotation * (used - fixed)) % max(1, count - fixed)
        return jnp.zeros((count,), jnp.int32).at[order[jnp.where(places < fixed, places, moved)]].set(jnp.asarray(tallies, jnp.int32))

    tallies = jnp.where(number % 4 == 0, named(packed, number // 4), named(common, number - number // 4 - 1))
    mixed = jax.random.permutation(jax.random.fold_in(own, 3), count)
    giver, sink = mixed[0:count // 2 * 2:2], mixed[1:count // 2 * 2:2]
    slack = jnp.minimum(tallies[giver] - 1, most - tallies[sink]) // 2
    slack = jnp.where((giver == order[0]) | (sink == order[0]) | (tallies[sink] == 0), 0, jnp.maximum(slack, 0))
    moved = jax.random.randint(jax.random.fold_in(own, 4), (count // 2,), 0, 1 << 20) % (slack + 1)
    tallies = tallies.at[giver].add(-moved).at[sink].add(moved)
    members = jnp.searchsorted(jnp.cumsum(tallies), jnp.arange(rows * top), side="right").astype(jnp.int32)
    table = members.reshape(top, rows).T
    table = table[jax.random.permutation(jax.random.fold_in(own, 1), rows)]
    rotation = jax.random.randint(jax.random.fold_in(own, 2), (rows, 1), 0, top)
    return jnp.take_along_axis(table, (jnp.arange(top)[None, :] + rotation) % top, axis=1)


def portions_of(number_of, total, most, skew, full):
    weights = [(1 << 20) // math.isqrt(standing ** skew) + 1 for standing in range(1, number_of + 1)]
    largest = most if full else min(most, max(-(-total // number_of), total * weights[0] // sum(weights)))
    least = 1 if total - largest >= number_of - 1 else 0
    holding, surplus = [largest] + [least] * (number_of - 1), total - largest - least * (number_of - 1)
    while surplus > 0:
        free = [i for i in range(1, number_of) if holding[i] < largest] or [i for i in range(1, number_of) if holding[i] < most]
        pool, budget = sum([weights[i] for i in free]), surplus
        for i in free:
            more = min(most - holding[i], max(1, budget * weights[i] // pool), surplus)
            holding[i] = holding[i] + more
            surplus = surplus - more
    return np.array(holding)


def noise(rng, shape, deviation, limit, cuts=(), held_as=jnp.bfloat16):
    gain = block_levels(rng, shape, cuts, -0.22, 0.18) if cuts else 1.0
    drawn = jax.random.normal(rng, shape, jnp.float32) * deviation * gain
    return jnp.minimum(jnp.maximum(drawn, -limit), limit).astype(held_as)


def setup_inputs(seed: int = 0) -> dict:
    splits = jax.random.split(jax.random.key(seed), 8)
    table = noise(splits[0], (VOCAB, D), 1.0, 6.0, ((0, 32),))
    owner_keys = jax.random.split(jax.random.fold_in(splits[1], 1), GROUPS * ROWS // ROWS)
    owner_turns = jax.random.permutation(jax.random.fold_in(splits[1], 3), GROUPS * ROWS // ROWS)
    owner = jax.vmap(lambda own, number: shared_out(jax.random.fold_in(splits[1], 2), own, number, ROWS, N_TABLE, 1, CAP, 2))(owner_keys, owner_turns).reshape((GROUPS, ROWS, 1))
    row_in_shard = plant(jax.random.randint(splits[2], (GROUPS, ROWS), 0, VOCAB_DEV), jax.random.fold_in(splits[2], 1), 0, VOCAB_DEV - 1).astype(jnp.int32)
    segment = jax.vmap(lambda own: jnp.searchsorted(jnp.cumsum(uneven(own, NSEG, ROWS, MOST, 2)), jnp.arange(ROWS), side="right"))(jax.random.split(splits[3], GROUPS)).reshape((GROUPS, ROWS)).astype(jnp.int32)
    w_in = noise(splits[4], (D, 4 * D), D ** -0.5, 0.25)
    w_out = noise(splits[5], (D, D), D ** -0.5, 0.25)
    cotangent = noise(splits[6], (GROUPS, ROWS, D), 1.0, 6.0, ((0, 32),))
    return {"table": table, "owner": owner, "row_in_shard": row_in_shard, "segment": segment, "w_in": w_in, "w_out": w_out, "cotangent": cotangent}


EPS = 1e-05

def normalize(values):
    average = lax.optimization_barrier(jnp.mean(values, axis=-1, keepdims=True))
    centred = values - average
    spread = lax.optimization_barrier(jnp.mean(centred * centred, axis=-1, keepdims=True))
    return centred * lax.rsqrt(spread + EPS)

def hstu_layer(embedded, w_in, w_out, segment):
    row_count, width = embedded.shape
    head_size = width // HEADS
    normed = normalize(embedded.astype(jnp.float32)).astype(jnp.bfloat16)
    mixed_all = jax.nn.silu(jnp.dot(normed, w_in, preferred_element_type=jnp.float32)).astype(jnp.bfloat16)
    gate_part = mixed_all[:, :width]
    value_part = mixed_all[:, width:2 * width].reshape(row_count, HEADS, head_size)
    query_part = mixed_all[:, 2 * width:3 * width].reshape(row_count, HEADS, head_size)
    key_part = mixed_all[:, 3 * width:].reshape(row_count, HEADS, head_size)
    position = jnp.arange(row_count)
    allowed = (segment[:, None] == segment[None, :]) & (position[None, :] <= position[:, None])
    scores = jnp.einsum('qhd,khd->hqk', query_part.astype(jnp.float32), key_part.astype(jnp.float32)) * head_size ** (-0.5)
    weights = jnp.where(allowed[None], jax.nn.silu(scores), 0.0).astype(jnp.bfloat16)
    attended = jnp.einsum('hqk,khd->qhd', weights.astype(jnp.float32), value_part.astype(jnp.float32)).reshape(row_count, width)
    gated = (normalize(attended) * gate_part.astype(jnp.float32)).astype(jnp.bfloat16)
    result = embedded.astype(jnp.float32) + jnp.dot(gated, w_out, preferred_element_type=jnp.float32)
    return result.astype(jnp.bfloat16)

def reference(table, owner, row_in_shard, segment, w_in, w_out, cotangent):
    item_index = (owner[:, :, 0] * VOCAB_DEV + row_in_shard).astype(jnp.int32)
    embedded = jnp.take(table, item_index, axis=0)

    def per_group(carry, inputs):
        emb_rows, seg_rows, cot_rows = inputs

        def local_layer(emb_in, weight_in, weight_out):
            return hstu_layer(emb_in, weight_in, weight_out, seg_rows)
        layer_rows, pullback = jax.vjp(local_layer, emb_rows, w_in, w_out)
        d_emb, d_in, d_out = pullback(cot_rows)
        return ((carry[0] + d_in.astype(jnp.float32), carry[1] + d_out.astype(jnp.float32)), (layer_rows, d_emb))
    start = (jnp.zeros(w_in.shape, jnp.float32), jnp.zeros(w_out.shape, jnp.float32))
    (grad_w_in, grad_w_out), (layer_out, d_emb) = lax.scan(per_group, start, (embedded, segment, cotangent))
    grad_table = jnp.zeros(table.shape, jnp.float32).at[item_index.reshape(-1)].add(d_emb.reshape(-1, table.shape[1]).astype(jnp.float32))
    return (layer_out, grad_table, grad_w_in, grad_w_out)
```

```python
import jax
import jax.numpy as jnp
from jax import lax
from jax.sharding import PartitionSpec as P

HEADS = 8


EPS = 1e-05


def normalize(values):
    average = jnp.mean(values, axis=-1, keepdims=True)
    centred = values - average
    spread = jnp.mean(centred * centred, axis=-1, keepdims=True)
    return centred * lax.rsqrt(spread + EPS)


def hstu_layer(embedded, w_in, w_out, segment):
    row_count, width = embedded.shape
    head_size = width // HEADS
    normed = normalize(embedded.astype(jnp.float32)).astype(jnp.bfloat16)
    mixed_all = jax.nn.silu(jnp.dot(normed, w_in, preferred_element_type=jnp.float32)).astype(
        jnp.bfloat16
    )
    gate_part = mixed_all[:, :width]
    value_part = mixed_all[:, width : 2 * width].reshape(row_count, HEADS, head_size)
    query_part = mixed_all[:, 2 * width : 3 * width].reshape(row_count, HEADS, head_size)
    key_part = mixed_all[:, 3 * width :].reshape(row_count, HEADS, head_size)
    position = jnp.arange(row_count)
    allowed = (segment[:, None] == segment[None, :]) & (position[None, :] <= position[:, None])
    scores = jnp.einsum(
        "qhd,khd->hqk", query_part, key_part, preferred_element_type=jnp.float32
    ) * head_size ** (-0.5)
    weights = jnp.where(allowed[None], jax.nn.silu(scores), 0.0).astype(jnp.bfloat16)
    attended = jnp.einsum(
        "hqk,khd->qhd", weights, value_part, preferred_element_type=jnp.float32
    ).reshape(row_count, width)
    gated = (normalize(attended) * gate_part.astype(jnp.float32)).astype(jnp.bfloat16)
    result = embedded.astype(jnp.float32) + jnp.dot(
        gated, w_out, preferred_element_type=jnp.float32
    )
    return result.astype(jnp.bfloat16)


def on_device(table, owner, row_in_shard, segment, w_in, w_out, cotangent):
    shards = lax.axis_size("table")
    row_count = owner.shape[1]
    capacity = 2 * row_count // shards
    slot_total = shards * capacity
    vocab_rows = table.shape[0]
    target = owner[0, :, 0]
    local_row = row_in_shard[0]
    positions = jnp.arange(row_count)
    earlier = (target[None, :] == target[:, None]) & (positions[None, :] < positions[:, None])
    rank_own = jnp.sum(earlier.astype(jnp.int32), axis=1)
    slot_index = target * capacity + rank_own
    slot_match = slot_index[None, :] == jnp.arange(slot_total)[:, None]
    filled = jnp.any(slot_match, axis=1)
    source_row = jnp.sum(jnp.where(slot_match, jnp.arange(row_count)[None, :], 0), axis=1)
    request = jnp.where(filled, jnp.take(local_row, source_row), -1).reshape(shards, capacity)
    asked_rows = lax.all_to_all(request, "table", split_axis=0, concat_axis=0, tiled=True)
    is_valid = asked_rows >= 0
    found_rows = jnp.take(table, jnp.maximum(asked_rows, 0).reshape(-1), axis=0).reshape(
        shards, capacity, -1
    )
    found_rows = jnp.where(is_valid[..., None], found_rows, jnp.zeros((), table.dtype))
    returned = lax.all_to_all(found_rows, "table", split_axis=0, concat_axis=0, tiled=True)
    embedded = jnp.take(returned.reshape(slot_total, -1), slot_index, axis=0)
    seg_rows = segment[0]

    def local_layer(emb_in, weight_in, weight_out):
        return hstu_layer(emb_in, weight_in, weight_out, seg_rows)

    layer_rows, pullback = jax.vjp(local_layer, embedded, w_in, w_out)
    d_emb, d_in, d_out = pullback(cotangent[0])
    sent_grads = jnp.where(
        filled[:, None], jnp.take(d_emb, source_row, axis=0), jnp.zeros((), d_emb.dtype)
    )
    arrived = lax.all_to_all(
        sent_grads.reshape(shards, capacity, -1), "table", split_axis=0, concat_axis=0, tiled=True
    )
    flat_grads = arrived.reshape(slot_total, -1)
    table_ids = jnp.where(is_valid, asked_rows, vocab_rows).reshape(-1)
    partial_sum = jax.ops.segment_sum(
        flat_grads.astype(jnp.float32), table_ids, num_segments=vocab_rows + 1
    )[:vocab_rows]
    grad_table = lax.psum(partial_sum.astype(jnp.bfloat16), "dp").astype(jnp.float32)
    share_in, share_out = (
        lax.psum_scatter(
            d_in.astype(jnp.float32).astype(jnp.bfloat16), "dp", scatter_dimension=1, tiled=True
        ).astype(jnp.float32),
        lax.psum_scatter(
            d_out.astype(jnp.float32).astype(jnp.bfloat16), "dp", scatter_dimension=0, tiled=True
        ).astype(jnp.float32),
    )
    grad_w_in, grad_w_out = lax.psum((share_in, share_out), "table")
    return (layer_rows[None], grad_table, grad_w_in, grad_w_out)


def solution(mesh):
    placed = (
        P("table", None),
        P(("table", "dp"), None, None),
        P(("table", "dp"), None),
        P(("table", "dp"), None),
        P(),
        P(),
        P(("table", "dp"), None, None),
    )
    return jax.shard_map(
        on_device,
        mesh=mesh,
        in_specs=placed,
        out_specs=(P(("table", "dp"), None, None), P("table", None), P(None, "dp"), P("dp", None)),
        check_vma=False,
    )
```

```python
import functools

import jax
import jax.numpy as jnp
from jax import lax
from jax.experimental import pallas as pl
from jax.experimental.pallas import tpu as pltpu
from jax.sharding import PartitionSpec as P

HEADS = 8


EPS = 1e-05


def normalize(values):
    average = jnp.mean(values, axis=-1, keepdims=True)
    centred = values - average
    spread = jnp.mean(centred * centred, axis=-1, keepdims=True)
    return centred * lax.rsqrt(spread + EPS)


def hstu_layer(embedded, w_in, w_out, segment):
    row_count, width = embedded.shape
    head_size = width // HEADS
    normed = normalize(embedded.astype(jnp.float32)).astype(jnp.bfloat16)
    mixed_all = jax.nn.silu(jnp.dot(normed, w_in, preferred_element_type=jnp.float32)).astype(
        jnp.bfloat16
    )
    gate_part = mixed_all[:, :width]
    value_part = mixed_all[:, width : 2 * width].reshape(row_count, HEADS, head_size)
    query_part = mixed_all[:, 2 * width : 3 * width].reshape(row_count, HEADS, head_size)
    key_part = mixed_all[:, 3 * width :].reshape(row_count, HEADS, head_size)
    position = jnp.arange(row_count)
    allowed = (segment[:, None] == segment[None, :]) & (position[None, :] <= position[:, None])
    scores = jnp.einsum(
        "qhd,khd->hqk", query_part, key_part, preferred_element_type=jnp.float32
    ) * head_size ** (-0.5)
    weights = jnp.where(allowed[None], jax.nn.silu(scores), 0.0).astype(jnp.bfloat16)
    attended = jnp.einsum(
        "hqk,khd->qhd", weights, value_part, preferred_element_type=jnp.float32
    ).reshape(row_count, width)
    gated = (normalize(attended) * gate_part.astype(jnp.float32)).astype(jnp.bfloat16)
    result = embedded.astype(jnp.float32) + jnp.dot(
        gated, w_out, preferred_element_type=jnp.float32
    )
    return result.astype(jnp.bfloat16)


def share_parts(wide, narrow):
    third = (wide + narrow) // 3 // 128 * 128 + 128
    rest = wide - 2 * third
    return (
        (0, 0, third, 0, 0),
        (0, third, third, third, 1),
        (0, 2 * third, rest, 2 * third, 2),
        (1, 0, narrow, wide, 2),
    )


def sum_shares_kernel(
    shards, parts, in_ref, out_ref, sum_in_ref, sum_out_ref,
    work, landing, gathered, send_sem, recv_sem, back_send_sem, back_recv_sem,
):
    rows, wide = in_ref.shape
    me = lax.axis_index("table")
    levels = shards.bit_length() - 1
    sources = (in_ref, out_ref)

    def side(bit):
        return (me // (1 << bit)) % 2

    def partner(bit):
        return me + (1 - 2 * side(bit)) * (1 << bit)

    barrier = pltpu.get_barrier_semaphore()
    for bit in range(levels):
        pl.semaphore_signal(
            barrier, inc=1, device_id={"table": partner(bit)}, device_id_type=pl.DeviceIdType.MESH
        )
    pl.semaphore_wait(barrier, levels)

    orders = []
    for part in parts:
        far = list(range(1, levels))
        orders.append([0] + far[part[4]:] + far[: part[4]])

    def rows_at(start, count):
        return pl.ds(pl.multiple_of(start, 16), count)

    bases = [[0] for _ in parts]

    def start_sum(p, step):
        source, first, columns, place, _ = parts[p]
        bit, half = orders[p][step], rows >> (step + 1)
        base = bases[p][step]
        bases[p].append(base + side(bit) * half)
        going = rows_at(base + (1 - side(bit)) * half, half)
        if step == 0:
            block = sources[source].at[going, pl.ds(first, columns)]
        else:
            block = work.at[going, pl.ds(place, columns)]
        copy = pltpu.make_async_remote_copy(
            src_ref=block,
            dst_ref=landing.at[pl.ds(rows - 2 * half, half), pl.ds(place, columns)],
            send_sem=send_sem.at[p, step],
            recv_sem=recv_sem.at[p, step],
            device_id={"table": partner(bit)},
            device_id_type=pl.DeviceIdType.MESH,
        )
        copy.start()
        return copy

    def start_back(p, step):
        _, _, columns, place, _ = parts[p]
        half = rows >> (step + 1)
        block = gathered.at[rows_at(bases[p][step + 1], half), pl.ds(place, columns)]
        copy = pltpu.make_async_remote_copy(
            src_ref=block,
            dst_ref=block,
            send_sem=back_send_sem.at[p, step],
            recv_sem=back_recv_sem.at[p, step],
            device_id={"table": partner(orders[p][step])},
            device_id_type=pl.DeviceIdType.MESH,
        )
        copy.start()
        return copy

    flying = [start_sum(p, 0) for p in range(len(parts))]
    for step in range(levels):
        half = rows >> (step + 1)
        for p, (source, first, columns, place, _) in enumerate(parts):
            flying[p].wait()
            kept = rows_at(bases[p][step + 1], half)
            here = slice(place, place + columns)
            if step == 0:
                own = sources[source][kept, first : first + columns]
            else:
                own = work[kept, here]
            other = landing[rows - 2 * half : rows - half, here]
            total = (own.astype(jnp.float32) + other.astype(jnp.float32)).astype(jnp.bfloat16)
            if step + 1 < levels:
                work[kept, here] = total
                flying[p] = start_sum(p, step + 1)
            else:
                gathered[kept, here] = total
                flying[p] = start_back(p, step)
    for step in reversed(range(levels)):
        for p in range(len(parts)):
            flying[p].wait()
            if step > 0:
                flying[p] = start_back(p, step - 1)
    sum_in_ref[...] = gathered[:, :wide]
    sum_out_ref[...] = gathered[:, wide:]


def sum_shares(shards, d_in, d_out):
    rows, wide = d_in.shape
    narrow = d_out.shape[1]
    parts = share_parts(wide, narrow)
    levels = shards.bit_length() - 1
    joined = (rows, wide + narrow)
    vmem = pl.BlockSpec(memory_space=pltpu.VMEM)
    sums = pl.pallas_call(
        functools.partial(sum_shares_kernel, shards, parts),
        out_shape=(
            jax.ShapeDtypeStruct(d_in.shape, jnp.bfloat16),
            jax.ShapeDtypeStruct(d_out.shape, jnp.bfloat16),
        ),
        in_specs=[vmem, vmem],
        out_specs=(vmem, vmem),
        scratch_shapes=[
            pltpu.VMEM(joined, jnp.bfloat16),
            pltpu.VMEM(joined, jnp.bfloat16),
            pltpu.VMEM(joined, jnp.bfloat16),
        ]
        + [pltpu.SemaphoreType.DMA((len(parts), levels))] * 4,
        compiler_params=pltpu.CompilerParams(
            collective_id=0, has_side_effects=True, vmem_limit_bytes=32 * 2**20
        ),
        cost_estimate=pl.CostEstimate(
            flops=rows * (wide + narrow), bytes_accessed=100 * 2**20, transcendentals=0
        ),
    )(d_in, d_out)
    return sums[0].astype(jnp.float32), sums[1].astype(jnp.float32)


def on_device(table, owner, row_in_shard, segment, w_in, w_out, cotangent):
    shards = lax.axis_size("table")
    row_count = owner.shape[1]
    capacity = 2 * row_count // shards
    slot_total = shards * capacity
    vocab_rows = table.shape[0]
    target = owner[0, :, 0]
    local_row = row_in_shard[0]
    positions = jnp.arange(row_count)
    earlier = (target[None, :] == target[:, None]) & (positions[None, :] < positions[:, None])
    rank_own = jnp.sum(earlier.astype(jnp.int32), axis=1)
    slot_index = target * capacity + rank_own
    slot_match = slot_index[None, :] == jnp.arange(slot_total)[:, None]
    filled = jnp.any(slot_match, axis=1)
    source_row = jnp.sum(jnp.where(slot_match, jnp.arange(row_count)[None, :], 0), axis=1)
    request = jnp.where(filled, jnp.take(local_row, source_row), -1).reshape(shards, capacity)
    asked_rows = lax.all_to_all(request, "table", split_axis=0, concat_axis=0, tiled=True)
    is_valid = asked_rows >= 0
    found_rows = jnp.take(table, jnp.maximum(asked_rows, 0).reshape(-1), axis=0).reshape(
        shards, capacity, -1
    )
    found_rows = jnp.where(is_valid[..., None], found_rows, jnp.zeros((), table.dtype))
    returned = lax.all_to_all(found_rows, "table", split_axis=0, concat_axis=0, tiled=True)
    embedded = jnp.take(returned.reshape(slot_total, -1), slot_index, axis=0)
    seg_rows = segment[0]

    def local_layer(emb_in, weight_in, weight_out):
        return hstu_layer(emb_in, weight_in, weight_out, seg_rows)

    layer_rows, pullback = jax.vjp(local_layer, embedded, w_in, w_out)
    d_emb, d_in, d_out = pullback(cotangent[0])
    sent_grads = jnp.where(
        filled[:, None], jnp.take(d_emb, source_row, axis=0), jnp.zeros((), d_emb.dtype)
    )
    arrived = lax.all_to_all(
        sent_grads.reshape(shards, capacity, -1), "table", split_axis=0, concat_axis=0, tiled=True
    )
    flat_grads = arrived.reshape(slot_total, -1)
    table_ids = jnp.where(is_valid, asked_rows, vocab_rows).reshape(-1)
    partial_sum = jax.ops.segment_sum(
        flat_grads.astype(jnp.float32), table_ids, num_segments=vocab_rows + 1
    )[:vocab_rows]
    grad_table = lax.psum(partial_sum.astype(jnp.bfloat16), "dp").astype(jnp.float32)
    copies = lax.axis_size("dp")
    rows = d_in.shape[0]
    if copies == 1 and shards & (shards - 1) == 0 and rows % (16 * shards) == 0:
        grad_w_in, grad_w_out = sum_shares(shards, d_in, d_out)
    else:
        share_in, share_out = (
            lax.psum_scatter(
                d_in.astype(jnp.float32).astype(jnp.bfloat16), "dp", scatter_dimension=1, tiled=True
            ).astype(jnp.float32),
            lax.psum_scatter(
                d_out.astype(jnp.float32).astype(jnp.bfloat16), "dp", scatter_dimension=0, tiled=True
            ).astype(jnp.float32),
        )
        grad_w_in, grad_w_out = lax.psum((share_in, share_out), "table")
    return (layer_rows[None], grad_table, grad_w_in, grad_w_out)


def solution(mesh):
    placed = (
        P("table", None),
        P(("table", "dp"), None, None),
        P(("table", "dp"), None),
        P(("table", "dp"), None),
        P(),
        P(),
        P(("table", "dp"), None, None),
    )
    return jax.shard_map(
        on_device,
        mesh=mesh,
        in_specs=placed,
        out_specs=(P(("table", "dp"), None, None), P("table", None), P(None, "dp"), P("dp", None)),
        check_vma=False,
    )
```

```python
import functools

import jax
import jax.numpy as jnp
from jax import lax
from jax.experimental import pallas as pl
from jax.experimental.pallas import tpu as pltpu
from jax.sharding import PartitionSpec as P

HEADS = 8


EPS = 1e-05


def normalize(values):
    average = jnp.mean(values, axis=-1, keepdims=True)
    centred = values - average
    spread = jnp.mean(centred * centred, axis=-1, keepdims=True)
    return centred * lax.rsqrt(spread + EPS)


def hstu_layer(embedded, w_in, w_out, segment):
    row_count, width = embedded.shape
    head_size = width // HEADS
    normed = normalize(embedded.astype(jnp.float32)).astype(jnp.bfloat16)
    mixed_all = jax.nn.silu(jnp.dot(normed, w_in, preferred_element_type=jnp.float32)).astype(
        jnp.bfloat16
    )
    gate_part = mixed_all[:, :width]
    value_part = mixed_all[:, width : 2 * width].reshape(row_count, HEADS, head_size)
    query_part = mixed_all[:, 2 * width : 3 * width].reshape(row_count, HEADS, head_size)
    key_part = mixed_all[:, 3 * width :].reshape(row_count, HEADS, head_size)
    position = jnp.arange(row_count)
    allowed = (segment[:, None] == segment[None, :]) & (position[None, :] <= position[:, None])
    scores = jnp.einsum(
        "qhd,khd->hqk", query_part, key_part, preferred_element_type=jnp.float32
    ) * head_size ** (-0.5)
    weights = jnp.where(allowed[None], jax.nn.silu(scores), 0.0).astype(jnp.bfloat16)
    attended = jnp.einsum(
        "hqk,khd->qhd", weights, value_part, preferred_element_type=jnp.float32
    ).reshape(row_count, width)
    gated = (normalize(attended) * gate_part.astype(jnp.float32)).astype(jnp.bfloat16)
    result = embedded.astype(jnp.float32) + jnp.dot(
        gated, w_out, preferred_element_type=jnp.float32
    )
    return result.astype(jnp.bfloat16)


def share_parts(wide, narrow):
    third = (wide + narrow) // 3 // 128 * 128 + 128
    rest = wide - 2 * third
    return (
        (0, 0, third, 0, 0),
        (0, third, third, third, 1),
        (0, 2 * third, rest, 2 * third, 2),
        (1, 0, narrow, wide, 2),
    )


def sum_shares_kernel(
    shards, parts, in_ref, out_ref, sum_in_ref, sum_out_ref,
    work, landing, gathered, send_sem, recv_sem, back_send_sem, back_recv_sem,
):
    rows, wide = in_ref.shape
    me = lax.axis_index("table")
    levels = shards.bit_length() - 1
    sources = (in_ref, out_ref)

    def side(bit):
        return (me // (1 << bit)) % 2

    def partner(bit):
        return me + (1 - 2 * side(bit)) * (1 << bit)

    barrier = pltpu.get_barrier_semaphore()
    for bit in range(levels):
        pl.semaphore_signal(
            barrier, inc=1, device_id={"table": partner(bit)}, device_id_type=pl.DeviceIdType.MESH
        )
    pl.semaphore_wait(barrier, levels)

    orders = []
    for part in parts:
        far = list(range(1, levels))
        orders.append([0] + far[part[4]:] + far[: part[4]])

    def rows_at(start, count):
        return pl.ds(pl.multiple_of(start, 16), count)

    bases = [[0] for _ in parts]

    def start_sum(p, step):
        source, first, columns, place, _ = parts[p]
        bit, half = orders[p][step], rows >> (step + 1)
        base = bases[p][step]
        bases[p].append(base + side(bit) * half)
        going = rows_at(base + (1 - side(bit)) * half, half)
        if step == 0:
            block = sources[source].at[going, pl.ds(first, columns)]
        else:
            block = work.at[going, pl.ds(place, columns)]
        copy = pltpu.make_async_remote_copy(
            src_ref=block,
            dst_ref=landing.at[pl.ds(rows - 2 * half, half), pl.ds(place, columns)],
            send_sem=send_sem.at[p, step],
            recv_sem=recv_sem.at[p, step],
            device_id={"table": partner(bit)},
            device_id_type=pl.DeviceIdType.MESH,
        )
        copy.start()
        return copy

    def start_back(p, step):
        _, _, columns, place, _ = parts[p]
        half = rows >> (step + 1)
        block = gathered.at[rows_at(bases[p][step + 1], half), pl.ds(place, columns)]
        copy = pltpu.make_async_remote_copy(
            src_ref=block,
            dst_ref=block,
            send_sem=back_send_sem.at[p, step],
            recv_sem=back_recv_sem.at[p, step],
            device_id={"table": partner(orders[p][step])},
            device_id_type=pl.DeviceIdType.MESH,
        )
        copy.start()
        return copy

    flying = [start_sum(p, 0) for p in range(len(parts))]
    for step in range(levels):
        half = rows >> (step + 1)
        for p, (source, first, columns, place, _) in enumerate(parts):
            flying[p].wait()
            kept = rows_at(bases[p][step + 1], half)
            here = slice(place, place + columns)
            if step == 0:
                own = sources[source][kept, first : first + columns]
            else:
                own = work[kept, here]
            other = landing[rows - 2 * half : rows - half, here]
            total = (own.astype(jnp.float32) + other.astype(jnp.float32)).astype(jnp.bfloat16)
            if step + 1 < levels:
                work[kept, here] = total
                flying[p] = start_sum(p, step + 1)
            else:
                gathered[kept, here] = total
                flying[p] = start_back(p, step)
    for step in reversed(range(levels)):
        for p in range(len(parts)):
            flying[p].wait()
            if step > 0:
                flying[p] = start_back(p, step - 1)
    sum_in_ref[...] = gathered[:, :wide]
    sum_out_ref[...] = gathered[:, wide:]


def sum_shares(shards, d_in, d_out):
    rows, wide = d_in.shape
    narrow = d_out.shape[1]
    parts = share_parts(wide, narrow)
    levels = shards.bit_length() - 1
    joined = (rows, wide + narrow)
    vmem = pl.BlockSpec(memory_space=pltpu.VMEM)
    sums = pl.pallas_call(
        functools.partial(sum_shares_kernel, shards, parts),
        out_shape=(
            jax.ShapeDtypeStruct(d_in.shape, jnp.bfloat16),
            jax.ShapeDtypeStruct(d_out.shape, jnp.bfloat16),
        ),
        in_specs=[vmem, vmem],
        out_specs=(vmem, vmem),
        scratch_shapes=[
            pltpu.VMEM(joined, jnp.bfloat16),
            pltpu.VMEM(joined, jnp.bfloat16),
            pltpu.VMEM(joined, jnp.bfloat16),
        ]
        + [pltpu.SemaphoreType.DMA((len(parts), levels))] * 4,
        compiler_params=pltpu.CompilerParams(
            collective_id=0, has_side_effects=True, vmem_limit_bytes=32 * 2**20
        ),
        cost_estimate=pl.CostEstimate(
            flops=rows * (wide + narrow), bytes_accessed=100 * 2**20, transcendentals=0
        ),
    )(d_in, d_out)
    return sums[0].astype(jnp.float32), sums[1].astype(jnp.float32)


def on_device(table, owner, row_in_shard, segment, w_in, w_out, cotangent):
    shards = lax.axis_size("table")
    row_count = owner.shape[1]
    capacity = 2 * row_count // shards
    slot_total = shards * capacity
    vocab_rows = table.shape[0]
    target = owner[0, :, 0]
    local_row = row_in_shard[0]
    positions = jnp.arange(row_count)
    earlier = (target[None, :] == target[:, None]) & (positions[None, :] < positions[:, None])
    rank_own = jnp.sum(earlier.astype(jnp.int32), axis=1)
    slot_index = target * capacity + rank_own
    slot_match = slot_index[None, :] == jnp.arange(slot_total)[:, None]
    source_row = jnp.sum(jnp.where(slot_match, jnp.arange(row_count)[None, :], 0), axis=1)
    request = jnp.sum(jnp.where(slot_match, local_row[None, :] + 1, 0), axis=1) - 1
    request = request.reshape(shards, capacity)
    asked_rows = lax.all_to_all(request, "table", split_axis=0, concat_axis=0, tiled=True)
    is_valid = asked_rows >= 0
    found_rows = jnp.take(table, jnp.maximum(asked_rows, 0).reshape(-1), axis=0).reshape(
        shards, capacity, -1
    )
    returned = lax.all_to_all(found_rows, "table", split_axis=0, concat_axis=0, tiled=True)
    embedded = jnp.take(returned.reshape(slot_total, -1), slot_index, axis=0)
    seg_rows = segment[0]

    def local_layer(emb_in, weight_in, weight_out):
        return hstu_layer(emb_in, weight_in, weight_out, seg_rows)

    layer_rows, pullback = jax.vjp(local_layer, embedded, w_in, w_out)
    d_emb, d_in, d_out = pullback(cotangent[0])
    sent_grads = jnp.take(d_emb, source_row, axis=0)
    arrived = lax.all_to_all(
        sent_grads.reshape(shards, capacity, -1), "table", split_axis=0, concat_axis=0, tiled=True
    )
    flat_grads = arrived.reshape(slot_total, -1)
    table_ids = jnp.where(is_valid, asked_rows, vocab_rows).reshape(-1)
    row_match = (table_ids[None, :] == jnp.arange(vocab_rows)[:, None]).astype(flat_grads.dtype)
    partial_sum = jnp.dot(row_match, flat_grads, preferred_element_type=jnp.float32)
    grad_table = lax.psum(partial_sum.astype(jnp.bfloat16), "dp").astype(jnp.float32)
    copies = lax.axis_size("dp")
    rows = d_in.shape[0]
    if copies == 1 and shards & (shards - 1) == 0 and rows % (16 * shards) == 0:
        grad_w_in, grad_w_out = sum_shares(shards, d_in, d_out)
    else:
        share_in, share_out = (
            lax.psum_scatter(
                d_in.astype(jnp.float32).astype(jnp.bfloat16), "dp", scatter_dimension=1, tiled=True
            ).astype(jnp.float32),
            lax.psum_scatter(
                d_out.astype(jnp.float32).astype(jnp.bfloat16), "dp", scatter_dimension=0, tiled=True
            ).astype(jnp.float32),
        )
        grad_w_in, grad_w_out = lax.psum((share_in, share_out), "table")
    return (layer_rows[None], grad_table, grad_w_in, grad_w_out)


def solution(mesh):
    placed = (
        P("table", None),
        P(("table", "dp"), None, None),
        P(("table", "dp"), None),
        P(("table", "dp"), None),
        P(),
        P(),
        P(("table", "dp"), None, None),
    )
    return jax.shard_map(
        on_device,
        mesh=mesh,
        in_specs=placed,
        out_specs=(P(("table", "dp"), None, None), P("table", None), P(None, "dp"), P("dp", None)),
        check_vma=False,
    )
```

```python
import functools

import jax
import jax.numpy as jnp
from jax import lax
from jax.experimental import pallas as pl
from jax.experimental.pallas import tpu as pltpu
from jax.sharding import PartitionSpec as P

HEADS = 8


EPS = 1e-05


def normalize(values):
    average = jnp.mean(values, axis=-1, keepdims=True)
    centred = values - average
    spread = jnp.mean(centred * centred, axis=-1, keepdims=True)
    return centred * lax.rsqrt(spread + EPS)


def hstu_layer(embedded, w_in, w_out, segment):
    row_count, width = embedded.shape
    head_size = width // HEADS
    normed = normalize(embedded.astype(jnp.float32)).astype(jnp.bfloat16)
    mixed_all = jax.nn.silu(jnp.dot(normed, w_in, preferred_element_type=jnp.float32)).astype(
        jnp.bfloat16
    )
    gate_part = mixed_all[:, :width]
    value_part = mixed_all[:, width : 2 * width].reshape(row_count, HEADS, head_size)
    query_part = mixed_all[:, 2 * width : 3 * width].reshape(row_count, HEADS, head_size)
    key_part = mixed_all[:, 3 * width :].reshape(row_count, HEADS, head_size)
    position = jnp.arange(row_count)
    allowed = (segment[:, None] == segment[None, :]) & (position[None, :] <= position[:, None])
    scores = jnp.einsum(
        "qhd,khd->hqk", query_part, key_part, preferred_element_type=jnp.float32
    ) * head_size ** (-0.5)
    weights = jnp.where(allowed[None], jax.nn.silu(scores), 0.0).astype(jnp.bfloat16)
    attended = jnp.einsum(
        "hqk,khd->qhd", weights, value_part, preferred_element_type=jnp.float32
    ).reshape(row_count, width)
    gated = (normalize(attended) * gate_part.astype(jnp.float32)).astype(jnp.bfloat16)
    result = embedded.astype(jnp.float32) + jnp.dot(
        gated, w_out, preferred_element_type=jnp.float32
    )
    return result.astype(jnp.bfloat16)


def share_parts(wide, narrow):
    third = (wide + narrow) // 3 // 128 * 128 + 128
    rest = wide - 2 * third
    return (
        (0, 0, third, 0, 0),
        (0, third, third, third, 1),
        (0, 2 * third, rest, 2 * third, 2),
        (1, 0, narrow, wide, 2),
    )


def sum_shares_kernel(
    shards, parts, in_ref, out_ref, sum_in_ref, sum_out_ref,
    work, landing, gathered, send_sem, recv_sem, back_send_sem, back_recv_sem,
):
    rows, wide = in_ref.shape
    me = lax.axis_index("table")
    levels = shards.bit_length() - 1
    sources = (in_ref, out_ref)

    def side(bit):
        return (me // (1 << bit)) % 2

    def partner(bit):
        return me + (1 - 2 * side(bit)) * (1 << bit)

    barrier = pltpu.get_barrier_semaphore()
    for bit in range(levels):
        pl.semaphore_signal(
            barrier, inc=1, device_id={"table": partner(bit)}, device_id_type=pl.DeviceIdType.MESH
        )
    pl.semaphore_wait(barrier, levels)

    orders = []
    for part in parts:
        far = list(range(1, levels))
        orders.append([0] + far[part[4]:] + far[: part[4]])

    def rows_at(start, count):
        return pl.ds(pl.multiple_of(start, 16), count)

    bases = [[0] for _ in parts]

    def start_sum(p, step):
        source, first, columns, place, _ = parts[p]
        bit, half = orders[p][step], rows >> (step + 1)
        base = bases[p][step]
        bases[p].append(base + side(bit) * half)
        going = rows_at(base + (1 - side(bit)) * half, half)
        if step == 0:
            block = sources[source].at[going, pl.ds(first, columns)]
        else:
            block = work.at[going, pl.ds(place, columns)]
        copy = pltpu.make_async_remote_copy(
            src_ref=block,
            dst_ref=landing.at[pl.ds(rows - 2 * half, half), pl.ds(place, columns)],
            send_sem=send_sem.at[p, step],
            recv_sem=recv_sem.at[p, step],
            device_id={"table": partner(bit)},
            device_id_type=pl.DeviceIdType.MESH,
        )
        copy.start()
        return copy

    def start_back(p, step):
        _, _, columns, place, _ = parts[p]
        half = rows >> (step + 1)
        block = gathered.at[rows_at(bases[p][step + 1], half), pl.ds(place, columns)]
        copy = pltpu.make_async_remote_copy(
            src_ref=block,
            dst_ref=block,
            send_sem=back_send_sem.at[p, step],
            recv_sem=back_recv_sem.at[p, step],
            device_id={"table": partner(orders[p][step])},
            device_id_type=pl.DeviceIdType.MESH,
        )
        copy.start()
        return copy

    flying = [start_sum(p, 0) for p in range(len(parts))]
    for step in range(levels):
        half = rows >> (step + 1)
        for p, (source, first, columns, place, _) in enumerate(parts):
            flying[p].wait()
            kept = rows_at(bases[p][step + 1], half)
            here = slice(place, place + columns)
            if step == 0:
                own = sources[source][kept, first : first + columns]
            else:
                own = work[kept, here]
            other = landing[rows - 2 * half : rows - half, here]
            total = (own.astype(jnp.float32) + other.astype(jnp.float32)).astype(jnp.bfloat16)
            if step + 1 < levels:
                work[kept, here] = total
                flying[p] = start_sum(p, step + 1)
            else:
                gathered[kept, here] = total
                flying[p] = start_back(p, step)
    for step in reversed(range(levels)):
        for p in range(len(parts)):
            flying[p].wait()
            if step > 0:
                flying[p] = start_back(p, step - 1)
    sum_in_ref[...] = gathered[:, :wide]
    sum_out_ref[...] = gathered[:, wide:]


def sum_shares(shards, d_in, d_out):
    rows, wide = d_in.shape
    narrow = d_out.shape[1]
    parts = share_parts(wide, narrow)
    levels = shards.bit_length() - 1
    joined = (rows, wide + narrow)
    vmem = pl.BlockSpec(memory_space=pltpu.VMEM)
    sums = pl.pallas_call(
        functools.partial(sum_shares_kernel, shards, parts),
        out_shape=(
            jax.ShapeDtypeStruct(d_in.shape, jnp.bfloat16),
            jax.ShapeDtypeStruct(d_out.shape, jnp.bfloat16),
        ),
        in_specs=[vmem, vmem],
        out_specs=(vmem, vmem),
        scratch_shapes=[
            pltpu.VMEM(joined, jnp.bfloat16),
            pltpu.VMEM(joined, jnp.bfloat16),
            pltpu.VMEM(joined, jnp.bfloat16),
        ]
        + [pltpu.SemaphoreType.DMA((len(parts), levels))] * 4,
        compiler_params=pltpu.CompilerParams(
            collective_id=0, has_side_effects=True, vmem_limit_bytes=32 * 2**20
        ),
        cost_estimate=pl.CostEstimate(
            flops=rows * (wide + narrow), bytes_accessed=100 * 2**20, transcendentals=0
        ),
    )(d_in, d_out)
    return sums[0].astype(jnp.float32), sums[1].astype(jnp.float32)


def pick(one_hot, rows, dim):
    picked = lax.dot_general(
        one_hot, rows, (((dim,), (0,)), ((), ())), preferred_element_type=jnp.float32
    )
    return picked.astype(rows.dtype)


def on_device(table, owner, row_in_shard, segment, w_in, w_out, cotangent):
    shards = lax.axis_size("table")
    row_count = owner.shape[1]
    capacity = 2 * row_count // shards
    slot_total = shards * capacity
    vocab_rows = table.shape[0]
    target = owner[0, :, 0]
    local_row = row_in_shard[0]
    positions = jnp.arange(row_count)
    earlier = (target[None, :] == target[:, None]) & (positions[None, :] < positions[:, None])
    rank_own = jnp.sum(earlier.astype(jnp.int32), axis=1)
    slot_index = target * capacity + rank_own
    slot_match = slot_index[None, :] == jnp.arange(slot_total)[:, None]
    request = jnp.sum(jnp.where(slot_match, local_row[None, :] + 1, 0), axis=1) - 1
    request = request.reshape(shards, capacity)
    asked_rows = lax.all_to_all(request, "table", split_axis=0, concat_axis=0, tiled=True)
    row_match = (jnp.arange(vocab_rows)[:, None] == asked_rows.reshape(-1)[None, :]).astype(
        table.dtype
    )
    slot_pick = slot_match.astype(table.dtype)
    found_rows = pick(row_match, table, 0).reshape(shards, capacity, -1)
    returned = lax.all_to_all(found_rows, "table", split_axis=0, concat_axis=0, tiled=True)
    embedded = pick(slot_pick, returned.reshape(slot_total, -1), 0)
    seg_rows = segment[0]

    def local_layer(emb_in, weight_in, weight_out):
        return hstu_layer(emb_in, weight_in, weight_out, seg_rows)

    layer_rows, pullback = jax.vjp(local_layer, embedded, w_in, w_out)
    d_emb, d_in, d_out = pullback(cotangent[0])
    sent_grads = pick(slot_pick, d_emb, 1)
    arrived = lax.all_to_all(
        sent_grads.reshape(shards, capacity, -1), "table", split_axis=0, concat_axis=0, tiled=True
    )
    flat_grads = arrived.reshape(slot_total, -1)
    partial_sum = jnp.dot(row_match, flat_grads, preferred_element_type=jnp.float32)
    grad_table = lax.psum(partial_sum.astype(jnp.bfloat16), "dp").astype(jnp.float32)
    copies = lax.axis_size("dp")
    rows = d_in.shape[0]
    if copies == 1 and shards & (shards - 1) == 0 and rows % (16 * shards) == 0:
        grad_w_in, grad_w_out = sum_shares(shards, d_in, d_out)
    else:
        share_in, share_out = (
            lax.psum_scatter(
                d_in.astype(jnp.float32).astype(jnp.bfloat16), "dp", scatter_dimension=1, tiled=True
            ).astype(jnp.float32),
            lax.psum_scatter(
                d_out.astype(jnp.float32).astype(jnp.bfloat16), "dp", scatter_dimension=0, tiled=True
            ).astype(jnp.float32),
        )
        grad_w_in, grad_w_out = lax.psum((share_in, share_out), "table")
    return (layer_rows[None], grad_table, grad_w_in, grad_w_out)


def solution(mesh):
    placed = (
        P("table", None),
        P(("table", "dp"), None, None),
        P(("table", "dp"), None),
        P(("table", "dp"), None),
        P(),
        P(),
        P(("table", "dp"), None, None),
    )
    return jax.shard_map(
        on_device,
        mesh=mesh,
        in_specs=placed,
        out_specs=(P(("table", "dp"), None, None), P("table", None), P(None, "dp"), P("dp", None)),
        check_vma=False,
    )
```

```python
import functools

import jax
import jax.numpy as jnp
from jax import lax
from jax.experimental import pallas as pl
from jax.experimental.pallas import tpu as pltpu
from jax.sharding import PartitionSpec as P

HEADS = 8


EPS = 1e-05


def normalize(values):
    average = jnp.mean(values, axis=-1, keepdims=True)
    centred = values - average
    spread = jnp.mean(centred * centred, axis=-1, keepdims=True)
    return centred * lax.rsqrt(spread + EPS)


def hstu_layer(embedded, w_in, w_out, segment):
    row_count, width = embedded.shape
    head_size = width // HEADS
    normed = normalize(embedded.astype(jnp.float32)).astype(jnp.bfloat16)
    mixed_all = jax.nn.silu(jnp.dot(normed, w_in, preferred_element_type=jnp.float32)).astype(
        jnp.bfloat16
    )
    gate_part = mixed_all[:, :width]
    value_part = mixed_all[:, width : 2 * width].reshape(row_count, HEADS, head_size)
    query_part = mixed_all[:, 2 * width : 3 * width].reshape(row_count, HEADS, head_size)
    key_part = mixed_all[:, 3 * width :].reshape(row_count, HEADS, head_size)
    position = jnp.arange(row_count)
    allowed = (segment[:, None] == segment[None, :]) & (position[None, :] <= position[:, None])
    scores = jnp.einsum(
        "qhd,khd->hqk", query_part, key_part, preferred_element_type=jnp.float32
    ) * head_size ** (-0.5)
    weights = jnp.where(allowed[None], jax.nn.silu(scores), 0.0).astype(jnp.bfloat16)
    attended = jnp.einsum(
        "hqk,khd->qhd", weights, value_part, preferred_element_type=jnp.float32
    ).reshape(row_count, width)
    gated = (normalize(attended) * gate_part.astype(jnp.float32)).astype(jnp.bfloat16)
    result = embedded.astype(jnp.float32) + jnp.dot(
        gated, w_out, preferred_element_type=jnp.float32
    )
    return result.astype(jnp.bfloat16)


def share_parts(wide, narrow):
    third = (wide + narrow) // 3 // 128 * 128 + 128
    rest = wide - 2 * third
    return (
        (0, 0, third, 0, 0),
        (0, third, third, third, 1),
        (0, 2 * third, rest, 2 * third, 2),
        (1, 0, narrow, wide, 2),
    )


def sum_shares_kernel(
    shards, parts, in_ref, out_ref, sum_in_ref, sum_out_ref,
    work, landing, gathered, send_sem, recv_sem, back_send_sem, back_recv_sem,
):
    rows, wide = in_ref.shape
    me = lax.axis_index("table")
    levels = shards.bit_length() - 1
    sources = (in_ref, out_ref)

    def side(bit):
        return (me // (1 << bit)) % 2

    def partner(bit):
        return me + (1 - 2 * side(bit)) * (1 << bit)

    barrier = pltpu.get_barrier_semaphore()
    for bit in range(levels):
        pl.semaphore_signal(
            barrier, inc=1, device_id={"table": partner(bit)}, device_id_type=pl.DeviceIdType.MESH
        )
    pl.semaphore_wait(barrier, levels)

    orders = []
    for part in parts:
        far = list(range(1, levels))
        orders.append([0] + far[part[4]:] + far[: part[4]])

    def rows_at(start, count):
        return pl.ds(pl.multiple_of(start, 16), count)

    bases = [[0] for _ in parts]

    def start_sum(p, step):
        source, first, columns, place, _ = parts[p]
        bit, half = orders[p][step], rows >> (step + 1)
        base = bases[p][step]
        bases[p].append(base + side(bit) * half)
        going = rows_at(base + (1 - side(bit)) * half, half)
        if step == 0:
            block = sources[source].at[going, pl.ds(first, columns)]
        else:
            block = work.at[going, pl.ds(place, columns)]
        copy = pltpu.make_async_remote_copy(
            src_ref=block,
            dst_ref=landing.at[pl.ds(rows - 2 * half, half), pl.ds(place, columns)],
            send_sem=send_sem.at[p, step],
            recv_sem=recv_sem.at[p, step],
            device_id={"table": partner(bit)},
            device_id_type=pl.DeviceIdType.MESH,
        )
        copy.start()
        return copy

    def start_back(p, step):
        _, _, columns, place, _ = parts[p]
        half = rows >> (step + 1)
        block = gathered.at[rows_at(bases[p][step + 1], half), pl.ds(place, columns)]
        copy = pltpu.make_async_remote_copy(
            src_ref=block,
            dst_ref=block,
            send_sem=back_send_sem.at[p, step],
            recv_sem=back_recv_sem.at[p, step],
            device_id={"table": partner(orders[p][step])},
            device_id_type=pl.DeviceIdType.MESH,
        )
        copy.start()
        return copy

    flying = [start_sum(p, 0) for p in range(len(parts))]
    for step in range(levels):
        half = rows >> (step + 1)
        for p, (source, first, columns, place, _) in enumerate(parts):
            flying[p].wait()
            kept = rows_at(bases[p][step + 1], half)
            here = slice(place, place + columns)
            if step == 0:
                own = sources[source][kept, first : first + columns]
            else:
                own = work[kept, here]
            other = landing[rows - 2 * half : rows - half, here]
            total = (own.astype(jnp.float32) + other.astype(jnp.float32)).astype(jnp.bfloat16)
            if step + 1 < levels:
                work[kept, here] = total
                flying[p] = start_sum(p, step + 1)
            else:
                gathered[kept, here] = total
                flying[p] = start_back(p, step)
    for step in reversed(range(levels)):
        for p in range(len(parts)):
            flying[p].wait()
            if step > 0:
                flying[p] = start_back(p, step - 1)
    sum_in_ref[...] = gathered[:, :wide]
    sum_out_ref[...] = gathered[:, wide:]


def sum_shares(shards, d_in, d_out):
    rows, wide = d_in.shape
    narrow = d_out.shape[1]
    parts = share_parts(wide, narrow)
    levels = shards.bit_length() - 1
    joined = (rows, wide + narrow)
    vmem = pl.BlockSpec(memory_space=pltpu.VMEM)
    sums = pl.pallas_call(
        functools.partial(sum_shares_kernel, shards, parts),
        out_shape=(
            jax.ShapeDtypeStruct(d_in.shape, jnp.bfloat16),
            jax.ShapeDtypeStruct(d_out.shape, jnp.bfloat16),
        ),
        in_specs=[vmem, vmem],
        out_specs=(vmem, vmem),
        scratch_shapes=[
            pltpu.VMEM(joined, jnp.bfloat16),
            pltpu.VMEM(joined, jnp.bfloat16),
            pltpu.VMEM(joined, jnp.bfloat16),
        ]
        + [pltpu.SemaphoreType.DMA((len(parts), levels))] * 4,
        compiler_params=pltpu.CompilerParams(
            collective_id=0, has_side_effects=True, vmem_limit_bytes=32 * 2**20
        ),
        cost_estimate=pl.CostEstimate(
            flops=rows * (wide + narrow), bytes_accessed=100 * 2**20, transcendentals=0
        ),
    )(d_in, d_out)
    return sums[0].astype(jnp.float32), sums[1].astype(jnp.float32)


def pick(one_hot, rows, dim):
    picked = lax.dot_general(
        one_hot, rows, (((dim,), (0,)), ((), ())), preferred_element_type=jnp.float32
    )
    return picked.astype(rows.dtype)


def on_device(table, owner, row_in_shard, segment, w_in, w_out, cotangent):
    shards = lax.axis_size("table")
    row_count = owner.shape[1]
    capacity = 2 * row_count // shards
    slot_total = shards * capacity
    vocab_rows = table.shape[0]
    target = owner[0, :, 0]
    local_row = row_in_shard[0]
    positions = jnp.arange(row_count)
    earlier = (target[None, :] == target[:, None]) & (positions[None, :] < positions[:, None])
    rank_own = jnp.sum(earlier.astype(jnp.int32), axis=1)
    slot_index = target * capacity + rank_own
    slot_match = slot_index[None, :] == jnp.arange(slot_total)[:, None]
    request = jnp.sum(jnp.where(slot_match, local_row[None, :] + 1, 0), axis=1) - 1
    request = request.reshape(shards, capacity)
    asked_rows = lax.all_to_all(request, "table", split_axis=0, concat_axis=0, tiled=True)
    row_match = (jnp.arange(vocab_rows)[:, None] == asked_rows.reshape(-1)[None, :]).astype(
        table.dtype
    )
    slot_pick = slot_match.astype(table.dtype)
    found_rows = pick(row_match, table, 0).reshape(shards, capacity, -1)
    returned = lax.all_to_all(found_rows, "table", split_axis=0, concat_axis=0, tiled=True)
    embedded = jnp.take(returned.reshape(slot_total, -1), slot_index, axis=0)
    seg_rows = segment[0]

    def local_layer(emb_in, weight_in, weight_out):
        return hstu_layer(emb_in, weight_in, weight_out, seg_rows)

    layer_rows, pullback = jax.vjp(local_layer, embedded, w_in, w_out)
    d_emb, d_in, d_out = pullback(cotangent[0])
    sent_grads = pick(slot_pick, d_emb, 1)
    arrived = lax.all_to_all(
        sent_grads.reshape(shards, capacity, -1), "table", split_axis=0, concat_axis=0, tiled=True
    )
    flat_grads = arrived.reshape(slot_total, -1)
    partial_sum = jnp.dot(row_match, flat_grads, preferred_element_type=jnp.float32)
    grad_table = lax.psum(partial_sum.astype(jnp.bfloat16), "dp").astype(jnp.float32)
    copies = lax.axis_size("dp")
    rows = d_in.shape[0]
    if copies == 1 and shards & (shards - 1) == 0 and rows % (16 * shards) == 0:
        grad_w_in, grad_w_out = sum_shares(shards, d_in, d_out)
    else:
        share_in, share_out = (
            lax.psum_scatter(
                d_in.astype(jnp.float32).astype(jnp.bfloat16), "dp", scatter_dimension=1, tiled=True
            ).astype(jnp.float32),
            lax.psum_scatter(
                d_out.astype(jnp.float32).astype(jnp.bfloat16), "dp", scatter_dimension=0, tiled=True
            ).astype(jnp.float32),
        )
        grad_w_in, grad_w_out = lax.psum((share_in, share_out), "table")
    return (layer_rows[None], grad_table, grad_w_in, grad_w_out)


def solution(mesh):
    placed = (
        P("table", None),
        P(("table", "dp"), None, None),
        P(("table", "dp"), None),
        P(("table", "dp"), None),
        P(),
        P(),
        P(("table", "dp"), None, None),
    )
    return jax.shard_map(
        on_device,
        mesh=mesh,
        in_specs=placed,
        out_specs=(P(("table", "dp"), None, None), P("table", None), P(None, "dp"), P("dp", None)),
        check_vma=False,
    )
```
